32 devices in a mesh: section: 4 (over y, x), dom: 8 (over z, core).
Axes of the slice: x: 2, y: 2, z: 4, core: 2. Of those that a mesh axis runs over, the one named last changes fastest.
Arguments:
- features: bfloat16 [2, 4096, 1024], P(None, 'dom'), may hold values from -6 to 6
- tiles: bfloat16 [2, 32, 12, 128, 128], P(None, 'dom'), may hold values from -0.15625 to 0.15625
- w_first: bfloat16 [4, 1024, 1024], P('section'), may hold values from -0.1875 to 0.1875
- w_second: bfloat16 [4, 1024, 1024], P('section'), may hold values from -0.1875 to 0.1875
- tile_block: int32 [2, 32, 12], replicated, may hold values from 0 to 63, as said below
Outputs:
- layer_outputs: bfloat16 [4, 2, 4096, 1024], P('section', None, 'dom')
The draws below stay inside these ranges and needn't reach their ends.
Inputs may be any that keep to these rules, and one draw needn't show every extreme that they name: `tile_block`: block row r belongs to partition r // 4 of a cycle of partitions. Entry [c, r, j] names a block of span c or an earlier span, owned by the partition of row r or by one of the two partitions beside it on the cycle. Among the 48 entries of one partition's block rows in one span, at most 6 name blocks of the partition one below and at most 6 name blocks of the partition one above, and one of these two counts is exactly 6 in every span and partition. Entries may repeat.
All inputs are finite; a program needn't handle non-finite values.
Results may differ from the reference program's by a relative error of at most 0.012.
Values may be sent and summed in bfloat16 or wider, within the bound.
A program may use at most 128 MiB of HBM per device.

```python
import jax
import jax.numpy as jnp
from jax import lax

F = 1024
TILE = 128
NT = 12
SPANS = 2
BR = 4
LAYERS = 4
K = 6
NBC = 32
VERTS = 4096


def draw_group(key, span_id, target):
    part_count = NBC // BR
    tiles_row = BR * NT
    key_dir, key_rest, key_mix, key_span, key_row = jax.random.split(key, 5)
    full_dir = jax.random.randint(key_dir, (), 0, 2).astype(jnp.int32)
    rest_pool = jnp.where(jnp.arange(tiles_row) < K, 1 - full_dir, 2).astype(jnp.int32)
    rest_pool = jax.random.permutation(key_rest, rest_pool)[:tiles_row - K]
    directions = jnp.concatenate([jnp.full((K,), full_dir, jnp.int32), rest_pool])
    directions = jax.random.permutation(key_mix, directions)
    offset_val = jnp.where(directions == 0, -1, jnp.where(directions == 1, 1, 0))
    owner = (target + offset_val) % part_count
    source_span = jax.random.randint(key_span, (tiles_row,), 0, span_id + 1)
    row_pick = jax.random.randint(key_row, (tiles_row,), 0, BR)
    global_ids = source_span * NBC + owner * BR + row_pick
    return global_ids.astype(jnp.int32).reshape(BR, NT)


def draw_tile_block(key, part):
    part_count = NBC // BR
    keys = jax.random.split(jax.random.fold_in(key, 7), SPANS * part_count)
    span_ids = jnp.repeat(jnp.arange(SPANS), part_count).astype(jnp.int32)
    targets = jnp.tile(jnp.arange(part_count), SPANS).astype(jnp.int32)
    grouped = jax.vmap(draw_group)(keys, span_ids, targets)
    return grouped.reshape(SPANS, NBC, NT)


def levels(own_key, dims, shards, smallest, top_value):
    def one(dim, parts):
        steps = jax.random.uniform(jax.random.fold_in(jax.random.fold_in(own_key, 6), dim), (parts,), jnp.float32, smallest / len(shards), top_value / len(shards))
        return jnp.repeat(jnp.exp(steps), dims[dim] // parts).reshape((-1,) + (1,) * (len(dims) - dim - 1))

    factor_of = one(*shards[0])
    for cut in shards[1:]:
        factor_of = factor_of * one(*cut)
    return factor_of


def normal_values(own_key, extent, deviation, most, shards=(), kind=jnp.bfloat16):
    values = deviation * jax.random.normal(own_key, extent, jnp.float32)
    if shards:
        values = values * levels(own_key, extent, shards, -0.22, 0.18)
    return jnp.clip(values, -most, most).astype(kind)


def setup_inputs(seed: int = 0) -> dict:
    key_of = jax.random.split(jax.random.key(seed), 6)
    return {
        "features": normal_values(key_of[0], (SPANS, VERTS, F), 1.0, 6.0, ((1, 8),)),
        "tiles": normal_values(key_of[1], (SPANS, NBC, NT, TILE, TILE), (NT * TILE) ** -0.5, 0.15625, ((1, 8),)),
        "w_first": normal_values(key_of[2], (LAYERS, F, F), F ** -0.5, 0.1875, ((0, 4),)),
        "w_second": normal_values(key_of[3], (LAYERS, F, F), F ** -0.5, 0.1875, ((0, 4),)),
        "tile_block": draw_tile_block(jax.random.fold_in(key_of[5], 71), 0),
    }


def reference(features, tiles, w_first, w_second, tile_block):
    current = features
    flat_ids = tile_block.reshape(-1, NT)
    flat_tiles = tiles.reshape(-1, NT, TILE, TILE)
    results = []
    for layer_idx in range(LAYERS):
        blocks = current.reshape(-1, TILE, F)

        def one_row(packed):
            block_ids, row_tiles = packed
            gathered = jnp.take(blocks, block_ids, axis=0)
            summed = jnp.einsum("jab,jbf->af", row_tiles.astype(jnp.float32), gathered.astype(jnp.float32))
            return summed.astype(jnp.bfloat16)

        agg_rows = lax.map(one_row, (flat_ids, flat_tiles)).reshape(-1, F)
        hidden = jax.nn.relu(jnp.dot(agg_rows, w_first[layer_idx], preferred_element_type=jnp.float32)).astype(jnp.bfloat16)
        updated = current.reshape(-1, F).astype(jnp.float32) + jnp.dot(hidden, w_second[layer_idx], preferred_element_type=jnp.float32)
        current = updated.astype(jnp.bfloat16).reshape(current.shape)
        results.append(current)
    return jnp.stack(results)
```

```python
import functools

import jax
import jax.numpy as jnp
from jax import lax
from jax.experimental import pallas as pl
from jax.experimental.pallas import tpu as pltpu
from jax.sharding import PartitionSpec as P

MESH = pl.DeviceIdType.MESH
CHUNK = 256
LAG = 2


def source_columns(tile_block, my_part, part_count, blk_rows):
    spans, nbc, _ = tile_block.shape
    ids = lax.dynamic_slice_in_dim(tile_block, my_part * blk_rows, blk_rows, 1)
    ids = ids.reshape(spans, -1)
    within = ids % nbc
    offset_val = (within // blk_rows - my_part) % part_count
    side = jnp.where(offset_val == part_count - 1, 1, jnp.where(offset_val == 1, 2, 0))
    return ((ids // nbc) * 3 + side) * blk_rows + within % blk_rows


def kernel(
    section_count, part_count, spans, nc,
    cols, feats, tiles, w_first, w_second, out,
    src, dense, tile_buf, w1_buf, w2_buf, acc, hidden, out_buf,
    feat_sem, tile_sem, w1_sem, w2_sem, out_sem,
    next_send, own_recv, up_send, low_recv, down_send, high_recv,
):
    blk_rows, tiles_row, tile_len = tiles.shape[1:4]
    rows = blk_rows * tile_len
    s = lax.axis_index("section")
    p = lax.axis_index("dom")
    after = {"section": lax.rem(s + 1, section_count)}
    before = {"section": lax.rem(s + section_count - 1, section_count)}
    above = {"dom": lax.rem(p + 1, part_count)}
    below = {"dom": lax.rem(p + part_count - 1, part_count)}
    first = s == 0
    last = s == section_count - 1

    def columns(k):
        return pl.ds(pl.multiple_of(k * CHUNK, CHUNK), CHUNK)

    def load_feats(c, k):
        return pltpu.make_async_copy(
            feats.at[c, :, columns(k)], src.at[c, k, 0], feat_sem.at[c, k]
        )

    def load_w1(k):
        return pltpu.make_async_copy(
            w_first.at[0, pl.ds(pl.multiple_of(k * CHUNK, CHUNK), CHUNK)],
            w1_buf.at[k],
            w1_sem.at[k],
        )

    def load_w2(k):
        return pltpu.make_async_copy(
            w_second.at[0, :, columns(k)], w2_buf.at[k], w2_sem.at[k]
        )

    def store_out(c, k):
        return pltpu.make_async_copy(
            out_buf.at[c, k], out.at[0, c, :, columns(k)], out_sem.at[c, k]
        )

    def to_next(c, k):
        return pltpu.make_async_remote_copy(
            src_ref=out_buf.at[c, k],
            dst_ref=src.at[c, k, 0],
            send_sem=next_send.at[c, k],
            recv_sem=own_recv.at[c, k],
            device_id=after,
            device_id_type=MESH,
        )

    def to_above(c, k):
        return pltpu.make_async_remote_copy(
            src_ref=src.at[c, k, 0],
            dst_ref=src.at[c, k, 1],
            send_sem=up_send.at[c, k],
            recv_sem=low_recv.at[c, k],
            device_id=above,
            device_id_type=MESH,
        )

    def to_below(c, k):
        return pltpu.make_async_remote_copy(
            src_ref=src.at[c, k, 0],
            dst_ref=src.at[c, k, 2],
            send_sem=down_send.at[c, k],
            recv_sem=high_recv.at[c, k],
            device_id=below,
            device_id_type=MESH,
        )

    @pl.when(first)
    def _():
        for c in range(spans):
            for k in range(nc):
                load_feats(c, k).start()

    load_tiles = pltpu.make_async_copy(tiles, tile_buf, tile_sem)
    load_tiles.start()
    for k in range(nc):
        load_w1(k).start()
        load_w2(k).start()

    barrier = pltpu.get_barrier_semaphore()
    pl.semaphore_signal(barrier, inc=1, device_id=above, device_id_type=MESH)
    pl.semaphore_signal(barrier, inc=1, device_id=below, device_id_type=MESH)

    @pl.when(jnp.logical_not(last))
    def _():
        pl.semaphore_signal(barrier, inc=1, device_id=after, device_id_type=MESH)

    @pl.when(jnp.logical_not(first))
    def _():
        pl.semaphore_signal(barrier, inc=1, device_id=before, device_id_type=MESH)

    pl.semaphore_wait(
        barrier,
        2 + jnp.where(first, 0, 1).astype(jnp.int32) + jnp.where(last, 0, 1).astype(jnp.int32),
    )

    def forward(c, k):
        @pl.when(first)
        def _():
            load_feats(c, k).wait()

        @pl.when(jnp.logical_not(first))
        def _():
            to_next(c, k).wait_recv()

        to_above(c, k).start()
        to_below(c, k).start()

    @pl.when(first)
    def _():
        for k in range(nc):
            forward(0, k)

    load_tiles.wait()
    for c in range(spans):
        blocks = (c + 1) * 3 * blk_rows

        @pl.loop(0, blk_rows)
        def _(r):
            @pl.loop(0, blocks)
            def _(n):
                total = jnp.zeros((tile_len, tile_len), jnp.float32)
                for j in range(tiles_row):
                    hit = jnp.where(cols[c, r * tiles_row + j] == n, 1.0, 0.0)
                    total += tile_buf[c, r, j].astype(jnp.float32) * hit
                dense[
                    c,
                    pl.ds(pl.multiple_of(r * tile_len, tile_len), tile_len),
                    pl.ds(pl.multiple_of(n * tile_len, tile_len), tile_len),
                ] = total.astype(jnp.bfloat16)

    for k in range(nc):
        load_w1(k).wait()
        load_w2(k).wait()

    for c in range(spans):
        acc[...] = jnp.zeros_like(acc)

        @pl.loop(0, nc + LAG)
        def _(k):
            @pl.when(jnp.logical_and(jnp.logical_not(first), k < nc))
            def _():
                forward(c, k)

            @pl.when(k >= LAG)
            def _():
                m = k - LAG
                to_above(c, m).wait_recv()
                to_below(c, m).wait_recv()
                agg = jnp.zeros((rows, CHUNK), jnp.float32)
                for e in range(c + 1):
                    agg += jnp.dot(
                        dense[c, :, e * 3 * rows:(e + 1) * 3 * rows],
                        src[e, m].reshape(3 * rows, CHUNK),
                        preferred_element_type=jnp.float32,
                    )
                acc[...] += jnp.dot(
                    agg.astype(jnp.bfloat16), w1_buf[m], preferred_element_type=jnp.float32
                )

        if c + 1 < spans:

            @pl.when(first)
            def _():
                for k in range(nc):
                    forward(c + 1, k)

        hidden[...] = jnp.maximum(acc[...], 0.0).astype(jnp.bfloat16)

        @pl.loop(0, nc)
        def _(k):
            updated = src[c, k, 0].astype(jnp.float32) + jnp.dot(
                hidden[...], w2_buf[k], preferred_element_type=jnp.float32
            )
            out_buf[c, k] = updated.astype(jnp.bfloat16)

            @pl.when(jnp.logical_not(last))
            def _():
                to_next(c, k).start()

            store_out(c, k).start()

    for c in range(spans):
        for k in range(nc):
            store_out(c, k).wait()
            to_above(c, k).wait_send()
            to_below(c, k).wait_send()

            @pl.when(jnp.logical_not(last))
            def _():
                to_next(c, k).wait_send()


def on_device(features, tiles, w_first, w_second, tile_block):
    spans, rows, feat = features.shape
    blk_rows, tiles_row, tile_len = tiles.shape[1:4]
    section_count = lax.axis_size("section")
    part_count = lax.axis_size("dom")
    nc = feat // CHUNK
    cols = source_columns(tile_block, lax.axis_index("dom"), part_count, blk_rows)
    chunk_sems = pltpu.SemaphoreType.DMA((spans, nc))
    bf16 = jnp.bfloat16
    anywhere = pl.BlockSpec(memory_space=pl.ANY)
    return pl.pallas_call(
        functools.partial(kernel, section_count, part_count, spans, nc),
        out_shape=jax.ShapeDtypeStruct((1, spans, rows, feat), bf16),
        in_specs=[pl.BlockSpec(memory_space=pltpu.SMEM)] + [anywhere] * 4,
        out_specs=anywhere,
        scratch_shapes=[
            pltpu.VMEM((spans, nc, 3, rows, CHUNK), bf16),
            pltpu.VMEM((spans, rows, spans * 3 * rows), bf16),
            pltpu.VMEM(tiles.shape, bf16),
            pltpu.VMEM((nc, CHUNK, feat), bf16),
            pltpu.VMEM((nc, feat, CHUNK), bf16),
            pltpu.VMEM((rows, feat), jnp.float32),
            pltpu.VMEM((rows, feat), bf16),
            pltpu.VMEM((spans, nc, rows, CHUNK), bf16),
            chunk_sems,
            pltpu.SemaphoreType.DMA,
            pltpu.SemaphoreType.DMA((nc,)),
            pltpu.SemaphoreType.DMA((nc,)),
        ]
        + [chunk_sems] * 7,
        compiler_params=pltpu.CompilerParams(
            collective_id=0, has_side_effects=True, vmem_limit_bytes=48 * 2**20
        ),
    )(cols, features, tiles, w_first, w_second)


def solution(mesh):
    placed = (
        P(None, "dom", None),
        P(None, "dom", None, None, None),
        P("section", None, None),
        P("section", None, None),
        P(),
    )
    return jax.shard_map(
        on_device,
        mesh=mesh,
        in_specs=placed,
        out_specs=P("section", None, "dom", None),
        check_vma=False,
    )
```

```python
import functools

import jax
import jax.numpy as jnp
from jax import lax
from jax.experimental import pallas as pl
from jax.experimental.pallas import tpu as pltpu
from jax.sharding import PartitionSpec as P

MESH = pl.DeviceIdType.MESH
CHUNK = 128
LAG = 3


def source_columns(tile_block, my_part, part_count, blk_rows):
    spans, nbc, _ = tile_block.shape
    ids = lax.dynamic_slice_in_dim(tile_block, my_part * blk_rows, blk_rows, 1)
    ids = ids.reshape(spans, -1)
    within = ids % nbc
    offset_val = (within // blk_rows - my_part) % part_count
    side = jnp.where(offset_val == part_count - 1, 1, jnp.where(offset_val == 1, 2, 0))
    return ((ids // nbc) * 3 + side) * blk_rows + within % blk_rows


def kernel(
    section_count, part_count, spans, nc,
    cols, feats, tiles, w_first, w_second, out,
    src, dense, tile_buf, w1_buf, w2_buf, acc, hidden, out_buf,
    feat_sem, tile_sem, w1_sem, w2_sem, out_sem,
    next_send, own_recv, up_send, low_recv, down_send, high_recv,
):
    blk_rows, tiles_row, tile_len = tiles.shape[1:4]
    rows = blk_rows * tile_len
    s = lax.axis_index("section")
    p = lax.axis_index("dom")
    after = {"section": lax.rem(s + 1, section_count)}
    before = {"section": lax.rem(s + section_count - 1, section_count)}
    above = {"dom": lax.rem(p + 1, part_count)}
    below = {"dom": lax.rem(p + part_count - 1, part_count)}
    first = s == 0
    last = s == section_count - 1

    def columns(k):
        return pl.ds(pl.multiple_of(k * CHUNK, CHUNK), CHUNK)

    def load_feats(c, k):
        return pltpu.make_async_copy(
            feats.at[c, :, columns(k)], src.at[c, k, 0], feat_sem.at[c, k]
        )

    def load_w1(k):
        return pltpu.make_async_copy(
            w_first.at[0, pl.ds(pl.multiple_of(k * CHUNK, CHUNK), CHUNK)],
            w1_buf.at[k],
            w1_sem.at[k],
        )

    def load_w2(k):
        return pltpu.make_async_copy(
            w_second.at[0, :, columns(k)], w2_buf.at[k], w2_sem.at[k]
        )

    def store_out(c, k):
        return pltpu.make_async_copy(
            out_buf.at[c, k], out.at[0, c, :, columns(k)], out_sem.at[c, k]
        )

    def to_next(c, k):
        return pltpu.make_async_remote_copy(
            src_ref=out_buf.at[c, k],
            dst_ref=src.at[c, k, 0],
            send_sem=next_send.at[c, k],
            recv_sem=own_recv.at[c, k],
            device_id=after,
            device_id_type=MESH,
        )

    def to_above(c, k):
        return pltpu.make_async_remote_copy(
            src_ref=src.at[c, k, 0],
            dst_ref=src.at[c, k, 1],
            send_sem=up_send.at[c, k],
            recv_sem=low_recv.at[c, k],
            device_id=above,
            device_id_type=MESH,
        )

    def to_below(c, k):
        return pltpu.make_async_remote_copy(
            src_ref=src.at[c, k, 0],
            dst_ref=src.at[c, k, 2],
            send_sem=down_send.at[c, k],
            recv_sem=high_recv.at[c, k],
            device_id=below,
            device_id_type=MESH,
        )

    @pl.when(first)
    def _():
        for c in range(spans):
            for k in range(nc):
                load_feats(c, k).start()

    load_tiles = pltpu.make_async_copy(tiles, tile_buf, tile_sem)
    load_tiles.start()
    for k in range(nc):
        load_w1(k).start()
        load_w2(k).start()

    barrier = pltpu.get_barrier_semaphore()
    pl.semaphore_signal(barrier, inc=1, device_id=above, device_id_type=MESH)
    pl.semaphore_signal(barrier, inc=1, device_id=below, device_id_type=MESH)

    @pl.when(jnp.logical_not(last))
    def _():
        pl.semaphore_signal(barrier, inc=1, device_id=after, device_id_type=MESH)

    @pl.when(jnp.logical_not(first))
    def _():
        pl.semaphore_signal(barrier, inc=1, device_id=before, device_id_type=MESH)

    pl.semaphore_wait(
        barrier,
        2 + jnp.where(first, 0, 1).astype(jnp.int32) + jnp.where(last, 0, 1).astype(jnp.int32),
    )

    def forward(c, k):
        @pl.when(first)
        def _():
            load_feats(c, k).wait()

        @pl.when(jnp.logical_not(first))
        def _():
            to_next(c, k).wait_recv()

        to_above(c, k).start()
        to_below(c, k).start()

    @pl.when(first)
    def _():
        for k in range(nc):
            forward(0, k)

    load_tiles.wait()
    for c in range(spans):
        blocks = (c + 1) * 3 * blk_rows

        @pl.loop(0, blk_rows)
        def _(r):
            @pl.loop(0, blocks)
            def _(n):
                total = jnp.zeros((tile_len, tile_len), jnp.float32)
                for j in range(tiles_row):
                    hit = jnp.where(cols[c, r * tiles_row + j] == n, 1.0, 0.0)
                    total += tile_buf[c, r, j].astype(jnp.float32) * hit
                dense[
                    c,
                    pl.ds(pl.multiple_of(r * tile_len, tile_len), tile_len),
                    pl.ds(pl.multiple_of(n * tile_len, tile_len), tile_len),
                ] = total.astype(jnp.bfloat16)

    for k in range(nc):
        load_w1(k).wait()
        load_w2(k).wait()

    for c in range(spans):
        acc[...] = jnp.zeros_like(acc)

        @pl.loop(0, nc + LAG)
        def _(k):
            @pl.when(jnp.logical_and(jnp.logical_not(first), k < nc))
            def _():
                forward(c, k)

            @pl.when(k >= LAG)
            def _():
                m = k - LAG
                to_above(c, m).wait_recv()
                to_below(c, m).wait_recv()
                agg = jnp.zeros((rows, CHUNK), jnp.float32)
                for e in range(c + 1):
                    agg += jnp.dot(
                        dense[c, :, e * 3 * rows:(e + 1) * 3 * rows],
                        src[e, m].reshape(3 * rows, CHUNK),
                        preferred_element_type=jnp.float32,
                    )
                acc[...] += jnp.dot(
                    agg.astype(jnp.bfloat16), w1_buf[m], preferred_element_type=jnp.float32
                )

        if c + 1 < spans:

            @pl.when(first)
            def _():
                for k in range(nc):
                    forward(c + 1, k)

        hidden[...] = jnp.maximum(acc[...], 0.0).astype(jnp.bfloat16)

        @pl.loop(0, nc)
        def _(k):
            updated = src[c, k, 0].astype(jnp.float32) + jnp.dot(
                hidden[...], w2_buf[k], preferred_element_type=jnp.float32
            )
            out_buf[c, k] = updated.astype(jnp.bfloat16)

            @pl.when(jnp.logical_not(last))
            def _():
                to_next(c, k).start()

            store_out(c, k).start()

    for c in range(spans):
        for k in range(nc):
            store_out(c, k).wait()
            to_above(c, k).wait_send()
            to_below(c, k).wait_send()

            @pl.when(jnp.logical_not(last))
            def _():
                to_next(c, k).wait_send()


def on_device(features, tiles, w_first, w_second, tile_block):
    spans, rows, feat = features.shape
    blk_rows, tiles_row, tile_len = tiles.shape[1:4]
    section_count = lax.axis_size("section")
    part_count = lax.axis_size("dom")
    nc = feat // CHUNK
    cols = source_columns(tile_block, lax.axis_index("dom"), part_count, blk_rows)
    chunk_sems = pltpu.SemaphoreType.DMA((spans, nc))
    bf16 = jnp.bfloat16
    anywhere = pl.BlockSpec(memory_space=pl.ANY)
    return pl.pallas_call(
        functools.partial(kernel, section_count, part_count, spans, nc),
        out_shape=jax.ShapeDtypeStruct((1, spans, rows, feat), bf16),
        in_specs=[pl.BlockSpec(memory_space=pltpu.SMEM)] + [anywhere] * 4,
        out_specs=anywhere,
        scratch_shapes=[
            pltpu.VMEM((spans, nc, 3, rows, CHUNK), bf16),
            pltpu.VMEM((spans, rows, spans * 3 * rows), bf16),
            pltpu.VMEM(tiles.shape, bf16),
            pltpu.VMEM((nc, CHUNK, feat), bf16),
            pltpu.VMEM((nc, feat, CHUNK), bf16),
            pltpu.VMEM((rows, feat), jnp.float32),
            pltpu.VMEM((rows, feat), bf16),
            pltpu.VMEM((spans, nc, rows, CHUNK), bf16),
            chunk_sems,
            pltpu.SemaphoreType.DMA,
            pltpu.SemaphoreType.DMA((nc,)),
            pltpu.SemaphoreType.DMA((nc,)),
        ]
        + [chunk_sems] * 7,
        compiler_params=pltpu.CompilerParams(
            collective_id=0, has_side_effects=True, vmem_limit_bytes=48 * 2**20
        ),
    )(cols, features, tiles, w_first, w_second)


def solution(mesh):
    placed = (
        P(None, "dom", None),
        P(None, "dom", None, None, None),
        P("section", None, None),
        P("section", None, None),
        P(),
    )
    return jax.shard_map(
        on_device,
        mesh=mesh,
        in_specs=placed,
        out_specs=P("section", None, "dom", None),
        check_vma=False,
    )
```

```python
import functools

import jax
import jax.numpy as jnp
from jax import lax
from jax.experimental import pallas as pl
from jax.experimental.pallas import tpu as pltpu
from jax.sharding import PartitionSpec as P

MESH = pl.DeviceIdType.MESH
CHUNK = 256
PIECES = 2


def source_columns(tile_block, my_part, part_count, blk_rows):
    spans, nbc, _ = tile_block.shape
    ids = lax.dynamic_slice_in_dim(tile_block, my_part * blk_rows, blk_rows, 1)
    ids = ids.reshape(spans, -1)
    within = ids % nbc
    offset_val = (within // blk_rows - my_part) % part_count
    side = jnp.where(offset_val == part_count - 1, 1, jnp.where(offset_val == 1, 2, 0))
    return ((ids // nbc) * 3 + side) * blk_rows + within % blk_rows


def kernel(
    section_count, part_count, spans, nc,
    cols, feats, tiles, w_first, w_second, out,
    src, dense, tile_buf, w1_buf, w2_buf, agg, acc, hidden, out_buf,
    feat_sem, tile_sem, w1_sem, w2_sem, out_sem,
    next_send, own_recv, up_send, low_recv, down_send, high_recv,
):
    blk_rows, tiles_row, tile_len = tiles.shape[1:4]
    rows = blk_rows * tile_len
    s = lax.axis_index("section")
    p = lax.axis_index("dom")
    after = {"section": lax.rem(s + 1, section_count)}
    before = {"section": lax.rem(s + section_count - 1, section_count)}
    above = {"dom": lax.rem(p + 1, part_count)}
    below = {"dom": lax.rem(p + part_count - 1, part_count)}
    first = s == 0
    last = s == section_count - 1

    def columns(k):
        return pl.ds(pl.multiple_of(k * CHUNK, CHUNK), CHUNK)

    piece_rows = rows // PIECES

    def piece(h):
        return pl.ds(pl.multiple_of(h * piece_rows, piece_rows), piece_rows)

    def load_feats(c, k, h):
        return pltpu.make_async_copy(
            feats.at[c, piece(h), columns(k)], src.at[c, k, 0, piece(h)], feat_sem.at[c, k, h]
        )

    def load_w1(k):
        return pltpu.make_async_copy(
            w_first.at[0, pl.ds(pl.multiple_of(k * CHUNK, CHUNK), CHUNK)],
            w1_buf.at[k],
            w1_sem.at[k],
        )

    def load_w2(k):
        return pltpu.make_async_copy(
            w_second.at[0, :, columns(k)], w2_buf.at[k], w2_sem.at[k]
        )

    def store_out(c, k):
        return pltpu.make_async_copy(
            out_buf.at[c, k], out.at[0, c, :, columns(k)], out_sem.at[c, k]
        )

    def to_next(c, k, h):
        return pltpu.make_async_remote_copy(
            src_ref=out_buf.at[c, k, piece(h)],
            dst_ref=src.at[c, k, 0, piece(h)],
            send_sem=next_send.at[c, k, h],
            recv_sem=own_recv.at[c, k, h],
            device_id=after,
            device_id_type=MESH,
        )

    def to_above(c, k, h):
        return pltpu.make_async_remote_copy(
            src_ref=src.at[c, k, 0, piece(h)],
            dst_ref=src.at[c, k, 1, piece(h)],
            send_sem=up_send.at[c, k, h],
            recv_sem=low_recv.at[c, k, h],
            device_id=above,
            device_id_type=MESH,
        )

    def to_below(c, k, h):
        return pltpu.make_async_remote_copy(
            src_ref=src.at[c, k, 0, piece(h)],
            dst_ref=src.at[c, k, 2, piece(h)],
            send_sem=down_send.at[c, k, h],
            recv_sem=high_recv.at[c, k, h],
            device_id=below,
            device_id_type=MESH,
        )

    @pl.when(first)
    def _():
        for c in range(spans):
            for k in range(nc):
                for h in range(PIECES):
                    load_feats(c, k, h).start()

    load_tiles = pltpu.make_async_copy(tiles, tile_buf, tile_sem)
    load_tiles.start()
    for k in range(nc):
        load_w1(k).start()
        load_w2(k).start()

    barrier = pltpu.get_barrier_semaphore()
    pl.semaphore_signal(barrier, inc=1, device_id=above, device_id_type=MESH)
    pl.semaphore_signal(barrier, inc=1, device_id=below, device_id_type=MESH)

    @pl.when(jnp.logical_not(last))
    def _():
        pl.semaphore_signal(barrier, inc=1, device_id=after, device_id_type=MESH)

    @pl.when(jnp.logical_not(first))
    def _():
        pl.semaphore_signal(barrier, inc=1, device_id=before, device_id_type=MESH)

    pl.semaphore_wait(
        barrier,
        2 + jnp.where(first, 0, 1).astype(jnp.int32) + jnp.where(last, 0, 1).astype(jnp.int32),
    )

    def forward(c, k):
        for h in range(PIECES):
            @pl.when(first)
            def _():
                load_feats(c, k, h).wait()

            @pl.when(jnp.logical_not(first))
            def _():
                to_next(c, k, h).wait_recv()

            to_above(c, k, h).start()
            to_below(c, k, h).start()

    @pl.when(first)
    def _():
        for k in range(nc):
            forward(0, k)

    load_tiles.wait()
    for c in range(spans):
        blocks = (c + 1) * 3 * blk_rows

        @pl.loop(0, blk_rows)
        def _(r):
            @pl.loop(0, blocks)
            def _(n):
                total = jnp.zeros((tile_len, tile_len), jnp.float32)
                for j in range(tiles_row):
                    hit = jnp.where(cols[c, r * tiles_row + j] == n, 1.0, 0.0)
                    total += tile_buf[c, r, j].astype(jnp.float32) * hit
                dense[
                    c,
                    pl.ds(pl.multiple_of(r * tile_len, tile_len), tile_len),
                    pl.ds(pl.multiple_of(n * tile_len, tile_len), tile_len),
                ] = total.astype(jnp.bfloat16)

    for k in range(nc):
        load_w1(k).wait()
        load_w2(k).wait()

    def finish(c, k):
        for h in range(PIECES):
            to_above(c, k, h).wait_recv()
            to_below(c, k, h).wait_recv()
        start = (3 * c + 1) * rows
        total = agg[...] + jnp.dot(
            dense[c, :, start:start + 2 * rows],
            src[c, k, 1:3].reshape(2 * rows, CHUNK),
            preferred_element_type=jnp.float32,
        )
        acc[...] += jnp.dot(
            total.astype(jnp.bfloat16), w1_buf[k], preferred_element_type=jnp.float32
        )

    def begin(c, k):
        total = jnp.dot(
            dense[c, :, 3 * c * rows:(3 * c + 1) * rows],
            src[c, k, 0],
            preferred_element_type=jnp.float32,
        )
        for e in range(c):
            total += jnp.dot(
                dense[c, :, 3 * e * rows:3 * (e + 1) * rows],
                src[e, k].reshape(3 * rows, CHUNK),
                preferred_element_type=jnp.float32,
            )
        agg[...] = total

    for c in range(spans):
        acc[...] = jnp.zeros_like(acc)

        @pl.loop(0, nc + 1)
        def _(k):
            @pl.when(jnp.logical_and(jnp.logical_not(first), k < nc))
            def _():
                forward(c, k)

            @pl.when(k >= 1)
            def _():
                finish(c, k - 1)

            @pl.when(k < nc)
            def _():
                begin(c, k)

        if c + 1 < spans:

            @pl.when(first)
            def _():
                for k in range(nc):
                    forward(c + 1, k)

        hidden[...] = jnp.maximum(acc[...], 0.0).astype(jnp.bfloat16)

        @pl.loop(0, nc)
        def _(k):
            updated = src[c, k, 0].astype(jnp.float32) + jnp.dot(
                hidden[...], w2_buf[k], preferred_element_type=jnp.float32
            )
            out_buf[c, k] = updated.astype(jnp.bfloat16)

            @pl.when(jnp.logical_not(last))
            def _():
                for h in range(PIECES):
                    to_next(c, k, h).start()

            store_out(c, k).start()

    for c in range(spans):
        for k in range(nc):
            store_out(c, k).wait()
            for h in range(PIECES):
                to_above(c, k, h).wait_send()
                to_below(c, k, h).wait_send()

                @pl.when(jnp.logical_not(last))
                def _():
                    to_next(c, k, h).wait_send()


def on_device(features, tiles, w_first, w_second, tile_block):
    spans, rows, feat = features.shape
    blk_rows, tiles_row, tile_len = tiles.shape[1:4]
    section_count = lax.axis_size("section")
    part_count = lax.axis_size("dom")
    nc = feat // CHUNK
    cols = source_columns(tile_block, lax.axis_index("dom"), part_count, blk_rows)
    chunk_sems = pltpu.SemaphoreType.DMA((spans, nc, PIECES))
    bf16 = jnp.bfloat16
    anywhere = pl.BlockSpec(memory_space=pl.ANY)
    return pl.pallas_call(
        functools.partial(kernel, section_count, part_count, spans, nc),
        out_shape=jax.ShapeDtypeStruct((1, spans, rows, feat), bf16),
        in_specs=[pl.BlockSpec(memory_space=pltpu.SMEM)] + [anywhere] * 4,
        out_specs=anywhere,
        scratch_shapes=[
            pltpu.VMEM((spans, nc, 3, rows, CHUNK), bf16),
            pltpu.VMEM((spans, rows, spans * 3 * rows), bf16),
            pltpu.VMEM(tiles.shape, bf16),
            pltpu.VMEM((nc, CHUNK, feat), bf16),
            pltpu.VMEM((nc, feat, CHUNK), bf16),
            pltpu.VMEM((rows, CHUNK), jnp.float32),
            pltpu.VMEM((rows, feat), jnp.float32),
            pltpu.VMEM((rows, feat), bf16),
            pltpu.VMEM((spans, nc, rows, CHUNK), bf16),
            chunk_sems,
            pltpu.SemaphoreType.DMA,
            pltpu.SemaphoreType.DMA((nc,)),
            pltpu.SemaphoreType.DMA((nc,)),
            pltpu.SemaphoreType.DMA((spans, nc)),
        ]
        + [chunk_sems] * 6,
        compiler_params=pltpu.CompilerParams(
            collective_id=0, has_side_effects=True, vmem_limit_bytes=48 * 2**20
        ),
    )(cols, features, tiles, w_first, w_second)


def solution(mesh):
    placed = (
        P(None, "dom", None),
        P(None, "dom", None, None, None),
        P("section", None, None),
        P("section", None, None),
        P(),
    )
    return jax.shard_map(
        on_device,
        mesh=mesh,
        in_specs=placed,
        out_specs=P("section", None, "dom", None),
        check_vma=False,
    )
```

```python
import functools

import jax
import jax.numpy as jnp
from jax import lax
from jax.experimental import pallas as pl
from jax.experimental.pallas import tpu as pltpu
from jax.sharding import PartitionSpec as P

MESH = pl.DeviceIdType.MESH
CHUNK = 256
PIECES = 2


def source_columns(tile_block, my_part, part_count, blk_rows):
    spans, nbc, _ = tile_block.shape
    ids = lax.dynamic_slice_in_dim(tile_block, my_part * blk_rows, blk_rows, 1)
    ids = ids.reshape(spans, -1)
    within = ids % nbc
    offset_val = (within // blk_rows - my_part) % part_count
    side = jnp.where(offset_val == part_count - 1, 1, jnp.where(offset_val == 1, 2, 0))
    return ((ids // nbc) * 3 + side) * blk_rows + within % blk_rows


def kernel(
    section_count, part_count, spans, nc,
    cols, feats, tiles, w_first, w_second, out,
    src, dense, tile_buf, w1_buf, w2_buf, agg, acc, hidden, out_buf, relay,
    feat_sem, tile_sem, w1_sem, w2_sem, out_sem,
    next_send, own_recv, up_send, low_recv, down_send, high_recv,
    wrap_send, wrap_recv, back_send,
):
    blk_rows, tiles_row, tile_len = tiles.shape[1:4]
    rows = blk_rows * tile_len
    s = lax.axis_index("section")
    p = lax.axis_index("dom")
    after = {"section": lax.rem(s + 1, section_count)}
    before = {"section": lax.rem(s + section_count - 1, section_count)}
    above = {"dom": lax.rem(p + 1, part_count)}
    below = {"dom": lax.rem(p + part_count - 1, part_count)}
    first = s == 0
    last = s == section_count - 1
    at_bottom = p == 0
    at_top = p == part_count - 1
    edge = jnp.logical_or(at_bottom, at_top)
    helpers = [1 + c % (section_count - 1) for c in range(spans)]
    sends_above = jnp.logical_not(jnp.logical_and(first, at_top))
    sends_below = jnp.logical_not(jnp.logical_and(first, at_bottom))

    def columns(k):
        return pl.ds(pl.multiple_of(k * CHUNK, CHUNK), CHUNK)

    piece_rows = rows // PIECES

    def piece(h):
        return pl.ds(pl.multiple_of(h * piece_rows, piece_rows), piece_rows)

    def load_feats(c, k, h):
        return pltpu.make_async_copy(
            feats.at[c, piece(h), columns(k)], src.at[c, k, 0, piece(h)], feat_sem.at[c, k, h]
        )

    def load_w1(k):
        return pltpu.make_async_copy(
            w_first.at[0, pl.ds(pl.multiple_of(k * CHUNK, CHUNK), CHUNK)],
            w1_buf.at[k],
            w1_sem.at[k],
        )

    def load_w2(k):
        return pltpu.make_async_copy(
            w_second.at[0, :, columns(k)], w2_buf.at[k], w2_sem.at[k]
        )

    def store_out(c, k):
        return pltpu.make_async_copy(
            out_buf.at[c, k], out.at[0, c, :, columns(k)], out_sem.at[c, k]
        )

    def to_next(c, k, h):
        return pltpu.make_async_remote_copy(
            src_ref=out_buf.at[c, k, piece(h)],
            dst_ref=src.at[c, k, 0, piece(h)],
            send_sem=next_send.at[c, k, h],
            recv_sem=own_recv.at[c, k, h],
            device_id=after,
            device_id_type=MESH,
        )

    def to_above(c, k, h):
        return pltpu.make_async_remote_copy(
            src_ref=src.at[c, k, 0, piece(h)],
            dst_ref=src.at[c, k, 1, piece(h)],
            send_sem=up_send.at[c, k, h],
            recv_sem=low_recv.at[c, k, h],
            device_id=above,
            device_id_type=MESH,
        )

    def to_below(c, k, h):
        return pltpu.make_async_remote_copy(
            src_ref=src.at[c, k, 0, piece(h)],
            dst_ref=src.at[c, k, 2, piece(h)],
            send_sem=down_send.at[c, k, h],
            recv_sem=high_recv.at[c, k, h],
            device_id=below,
            device_id_type=MESH,
        )

    def across(c, k, h):
        return pltpu.make_async_remote_copy(
            src_ref=feats.at[c, piece(h), columns(k)],
            dst_ref=relay.at[c, k, piece(h)],
            send_sem=wrap_send.at[c, k, h],
            recv_sem=wrap_recv.at[c, k, h],
            device_id={"dom": jnp.where(at_bottom, part_count - 1, 0)},
            device_id_type=MESH,
        )

    def back(c, k, h, side):
        return pltpu.make_async_remote_copy(
            src_ref=relay.at[c, k, piece(h)],
            dst_ref=src.at[c, k, side, piece(h)],
            send_sem=back_send.at[c, k, h],
            recv_sem=(low_recv if side == 1 else high_recv).at[c, k, h],
            device_id={"section": jnp.int32(0)},
            device_id_type=MESH,
        )

    @pl.when(first)
    def _():
        for c in range(spans):
            for k in range(nc):
                for h in range(PIECES):
                    load_feats(c, k, h).start()

    load_tiles = pltpu.make_async_copy(tiles, tile_buf, tile_sem)
    load_tiles.start()
    for k in range(nc):
        load_w1(k).start()
        load_w2(k).start()

    barrier = pltpu.get_barrier_semaphore()
    pl.semaphore_signal(barrier, inc=1, device_id=above, device_id_type=MESH)
    pl.semaphore_signal(barrier, inc=1, device_id=below, device_id_type=MESH)

    @pl.when(jnp.logical_not(last))
    def _():
        pl.semaphore_signal(barrier, inc=1, device_id=after, device_id_type=MESH)

    @pl.when(jnp.logical_not(first))
    def _():
        pl.semaphore_signal(barrier, inc=1, device_id=before, device_id_type=MESH)

    extra = sorted(set(helpers) - {1})
    for q in extra:
        @pl.when(jnp.logical_and(first, edge))
        def _():
            pl.semaphore_signal(
                barrier, inc=1, device_id={"section": jnp.int32(q)}, device_id_type=MESH
            )

        @pl.when(jnp.logical_and(s == q, edge))
        def _():
            pl.semaphore_signal(
                barrier, inc=1, device_id={"section": jnp.int32(0)}, device_id_type=MESH
            )

    def one_if(condition):
        return jnp.where(condition, 1, 0).astype(jnp.int32)

    peers = 2 + one_if(jnp.logical_not(first)) + one_if(jnp.logical_not(last))
    for q in extra:
        peers += one_if(jnp.logical_and(jnp.logical_or(first, s == q), edge))
    pl.semaphore_wait(barrier, peers)

    def forward(c, k):
        for h in range(PIECES):
            @pl.when(first)
            def _():
                load_feats(c, k, h).wait()

            @pl.when(jnp.logical_not(first))
            def _():
                to_next(c, k, h).wait_recv()

            @pl.when(sends_above)
            def _():
                to_above(c, k, h).start()

            @pl.when(sends_below)
            def _():
                to_below(c, k, h).start()

    @pl.when(first)
    def _():
        for k in range(nc):
            forward(0, k)

    pieces = [(k, h) for k in range(nc) for h in range(PIECES)]
    for c in range(spans):
        @pl.when(jnp.logical_and(s == helpers[c], edge))
        def _():
            for k, h in pieces:
                across(c, k, h).start()
            for k, h in pieces:
                across(c, k, h).wait_recv()

                @pl.when(at_bottom)
                def _():
                    back(c, k, h, 1).start()

                @pl.when(at_top)
                def _():
                    back(c, k, h, 2).start()

    load_tiles.wait()

    def build(c):
        blocks = (c + 1) * 3 * blk_rows

        @pl.loop(0, blk_rows)
        def _(r):
            @pl.loop(0, blocks)
            def _(n):
                total = jnp.zeros((tile_len, tile_len), jnp.float32)
                for j in range(tiles_row):
                    hit = jnp.where(cols[c, r * tiles_row + j] == n, 1.0, 0.0)
                    total += tile_buf[c, r, j].astype(jnp.float32) * hit
                dense[
                    c,
                    pl.ds(pl.multiple_of(r * tile_len, tile_len), tile_len),
                    pl.ds(pl.multiple_of(n * tile_len, tile_len), tile_len),
                ] = total.astype(jnp.bfloat16)

    build(0)

    @pl.when(jnp.logical_not(first))
    def _():
        for c in range(1, spans):
            build(c)

    for k in range(nc):
        load_w1(k).wait()
        load_w2(k).wait()

    def finish(c, k):
        for h in range(PIECES):
            to_above(c, k, h).wait_recv()
            to_below(c, k, h).wait_recv()
        start = (3 * c + 1) * rows
        total = agg[...] + jnp.dot(
            dense[c, :, start:start + 2 * rows],
            src[c, k, 1:3].reshape(2 * rows, CHUNK),
            preferred_element_type=jnp.float32,
        )
        acc[...] += jnp.dot(
            total.astype(jnp.bfloat16), w1_buf[k], preferred_element_type=jnp.float32
        )

    def begin(c, k):
        total = jnp.dot(
            dense[c, :, 3 * c * rows:(3 * c + 1) * rows],
            src[c, k, 0],
            preferred_element_type=jnp.float32,
        )
        for e in range(c):
            total += jnp.dot(
                dense[c, :, 3 * e * rows:3 * (e + 1) * rows],
                src[e, k].reshape(3 * rows, CHUNK),
                preferred_element_type=jnp.float32,
            )
        agg[...] = total

    for c in range(spans):
        if c > 0:
            @pl.when(first)
            def _():
                build(c)

        acc[...] = jnp.zeros_like(acc)

        @pl.loop(0, nc + 1)
        def _(k):
            @pl.when(jnp.logical_and(jnp.logical_not(first), k < nc))
            def _():
                forward(c, k)

            @pl.when(k >= 1)
            def _():
                finish(c, k - 1)

            @pl.when(k < nc)
            def _():
                begin(c, k)

        if c + 1 < spans:

            @pl.when(first)
            def _():
                for k in range(nc):
                    forward(c + 1, k)

        hidden[...] = jnp.maximum(acc[...], 0.0).astype(jnp.bfloat16)

        @pl.loop(0, nc)
        def _(k):
            updated = src[c, k, 0].astype(jnp.float32) + jnp.dot(
                hidden[...], w2_buf[k], preferred_element_type=jnp.float32
            )
            out_buf[c, k] = updated.astype(jnp.bfloat16)

            @pl.when(jnp.logical_not(last))
            def _():
                for h in range(PIECES):
                    to_next(c, k, h).start()

            store_out(c, k).start()

    for c in range(spans):
        for k in range(nc):
            store_out(c, k).wait()
            for h in range(PIECES):
                @pl.when(sends_above)
                def _():
                    to_above(c, k, h).wait_send()

                @pl.when(sends_below)
                def _():
                    to_below(c, k, h).wait_send()

                @pl.when(jnp.logical_and(s == helpers[c], edge))
                def _():
                    across(c, k, h).wait_send()
                    back(c, k, h, 1).wait_send()

                @pl.when(jnp.logical_not(last))
                def _():
                    to_next(c, k, h).wait_send()


def on_device(features, tiles, w_first, w_second, tile_block):
    spans, rows, feat = features.shape
    blk_rows, tiles_row, tile_len = tiles.shape[1:4]
    section_count = lax.axis_size("section")
    part_count = lax.axis_size("dom")
    nc = feat // CHUNK
    cols = source_columns(tile_block, lax.axis_index("dom"), part_count, blk_rows)
    chunk_sems = pltpu.SemaphoreType.DMA((spans, nc, PIECES))
    bf16 = jnp.bfloat16
    anywhere = pl.BlockSpec(memory_space=pl.ANY)
    return pl.pallas_call(
        functools.partial(kernel, section_count, part_count, spans, nc),
        out_shape=jax.ShapeDtypeStruct((1, spans, rows, feat), bf16),
        in_specs=[pl.BlockSpec(memory_space=pltpu.SMEM)] + [anywhere] * 4,
        out_specs=anywhere,
        scratch_shapes=[
            pltpu.VMEM((spans, nc, 3, rows, CHUNK), bf16),
            pltpu.VMEM((spans, rows, spans * 3 * rows), bf16),
            pltpu.VMEM(tiles.shape, bf16),
            pltpu.VMEM((nc, CHUNK, feat), bf16),
            pltpu.VMEM((nc, feat, CHUNK), bf16),
            pltpu.VMEM((rows, CHUNK), jnp.float32),
            pltpu.VMEM((rows, feat), jnp.float32),
            pltpu.VMEM((rows, feat), bf16),
            pltpu.VMEM((spans, nc, rows, CHUNK), bf16),
            pltpu.VMEM((spans, nc, rows, CHUNK), bf16),
            chunk_sems,
            pltpu.SemaphoreType.DMA,
            pltpu.SemaphoreType.DMA((nc,)),
            pltpu.SemaphoreType.DMA((nc,)),
            pltpu.SemaphoreType.DMA((spans, nc)),
        ]
        + [chunk_sems] * 9,
        compiler_params=pltpu.CompilerParams(
            collective_id=0, has_side_effects=True, vmem_limit_bytes=48 * 2**20
        ),
    )(cols, features, tiles, w_first, w_second)


def solution(mesh):
    placed = (
        P(None, "dom", None),
        P(None, "dom", None, None, None),
        P("section", None, None),
        P("section", None, None),
        P(),
    )
    return jax.shard_map(
        on_device,
        mesh=mesh,
        in_specs=placed,
        out_specs=P("section", None, "dom", None),
        check_vma=False,
    )
```

```python
import functools

import jax
import jax.numpy as jnp
from jax import lax
from jax.experimental import pallas as pl
from jax.experimental.pallas import tpu as pltpu
from jax.sharding import PartitionSpec as P

MESH = pl.DeviceIdType.MESH
CHUNK = 256
PIECES = 2


def source_columns(tile_block, my_part, part_count, blk_rows):
    spans, nbc, _ = tile_block.shape
    ids = lax.dynamic_slice_in_dim(tile_block, my_part * blk_rows, blk_rows, 1)
    ids = ids.reshape(spans, -1)
    within = ids % nbc
    offset_val = (within // blk_rows - my_part) % part_count
    side = jnp.where(offset_val == part_count - 1, 1, jnp.where(offset_val == 1, 2, 0))
    return ((ids // nbc) * 3 + side) * blk_rows + within % blk_rows


def kernel(
    section_count, part_count, spans, nc,
    cols, feats, tiles, w_first, w_second, out,
    src, dense, tile_buf, w1_buf, w2_buf, agg, acc, hidden, out_buf, relay, hop_buf,
    feat_sem, tile_sem, w1_sem, w2_sem, out_sem,
    next_send, own_recv, up_send, low_recv, down_send, high_recv,
    wrap_send, wrap_recv, back_send, hop_send, hop_recv,
):
    blk_rows, tiles_row, tile_len = tiles.shape[1:4]
    rows = blk_rows * tile_len
    s = lax.axis_index("section")
    p = lax.axis_index("dom")
    after = {"section": lax.rem(s + 1, section_count)}
    before = {"section": lax.rem(s + section_count - 1, section_count)}
    above = {"dom": lax.rem(p + 1, part_count)}
    below = {"dom": lax.rem(p + part_count - 1, part_count)}
    first = s == 0
    last = s == section_count - 1
    at_bottom = p == 0
    at_top = p == part_count - 1
    edge = jnp.logical_or(at_bottom, at_top)
    helpers = [1 + c % (section_count - 1) for c in range(spans)]
    rerouted = [(0, 1), (spans - 1, section_count - 1)] if section_count == 4 else []
    opposite = {"section": lax.rem(s + 2, section_count)}
    far_end = {"dom": jnp.where(at_bottom, part_count - 1, 0)}

    def direct(c):
        found = jnp.logical_not(first)
        for span, reached in rerouted:
            if span == c:
                found = jnp.logical_and(found, s != reached)
        return found

    def sends_above(c):
        return jnp.logical_or(direct(c), jnp.logical_not(at_top))

    def sends_below(c):
        return jnp.logical_or(direct(c), jnp.logical_not(at_bottom))


    def columns(k):
        return pl.ds(pl.multiple_of(k * CHUNK, CHUNK), CHUNK)

    piece_rows = rows // PIECES

    def piece(h):
        return pl.ds(pl.multiple_of(h * piece_rows, piece_rows), piece_rows)

    def load_feats(c, k, h):
        return pltpu.make_async_copy(
            feats.at[c, piece(h), columns(k)], src.at[c, k, 0, piece(h)], feat_sem.at[c, k, h]
        )

    def load_w1(k):
        return pltpu.make_async_copy(
            w_first.at[0, pl.ds(pl.multiple_of(k * CHUNK, CHUNK), CHUNK)],
            w1_buf.at[k],
            w1_sem.at[k],
        )

    def load_w2(k):
        return pltpu.make_async_copy(
            w_second.at[0, :, columns(k)], w2_buf.at[k], w2_sem.at[k]
        )

    def store_out(c, k):
        return pltpu.make_async_copy(
            out_buf.at[c, k], out.at[0, c, :, columns(k)], out_sem.at[c, k]
        )

    def to_next(c, k, h):
        return pltpu.make_async_remote_copy(
            src_ref=out_buf.at[c, k, piece(h)],
            dst_ref=src.at[c, k, 0, piece(h)],
            send_sem=next_send.at[c, k, h],
            recv_sem=own_recv.at[c, k, h],
            device_id=after,
            device_id_type=MESH,
        )

    def to_above(c, k, h):
        return pltpu.make_async_remote_copy(
            src_ref=src.at[c, k, 0, piece(h)],
            dst_ref=src.at[c, k, 1, piece(h)],
            send_sem=up_send.at[c, k, h],
            recv_sem=low_recv.at[c, k, h],
            device_id=above,
            device_id_type=MESH,
        )

    def to_below(c, k, h):
        return pltpu.make_async_remote_copy(
            src_ref=src.at[c, k, 0, piece(h)],
            dst_ref=src.at[c, k, 2, piece(h)],
            send_sem=down_send.at[c, k, h],
            recv_sem=high_recv.at[c, k, h],
            device_id=below,
            device_id_type=MESH,
        )

    def across(c, k, h):
        return pltpu.make_async_remote_copy(
            src_ref=feats.at[c, piece(h), columns(k)],
            dst_ref=relay.at[c, k, piece(h)],
            send_sem=wrap_send.at[c, k, h],
            recv_sem=wrap_recv.at[c, k, h],
            device_id=far_end,
            device_id_type=MESH,
        )

    def back(c, k, h, side):
        return pltpu.make_async_remote_copy(
            src_ref=relay.at[c, k, piece(h)],
            dst_ref=src.at[c, k, side, piece(h)],
            send_sem=back_send.at[c, k, h],
            recv_sem=(low_recv if side == 1 else high_recv).at[c, k, h],
            device_id={"section": jnp.int32(0)},
            device_id_type=MESH,
        )

    def hop(n, c, k, h, side=1):
        source = out_buf.at[c, k, piece(h)] if n == 0 else hop_buf.at[n - 1, k, piece(h)]
        if n < 3:
            target, arrival = hop_buf.at[n, k, piece(h)], hop_recv.at[n, k, h]
        else:
            target = src.at[c, k, side, piece(h)]
            arrival = (low_recv if side == 1 else high_recv).at[c, k, h]
        return pltpu.make_async_remote_copy(
            src_ref=source,
            dst_ref=target,
            send_sem=hop_send.at[n, k, h],
            recv_sem=arrival,
            device_id=(opposite, far_end, after, opposite)[n],
            device_id_type=MESH,
        )

    def takes_part(section):
        return jnp.logical_and(s == section % section_count, edge)

    def pass_on(c, reached):
        count = nc * PIECES

        @pl.when(takes_part(reached + 1))
        def _():
            @pl.loop(0, count + 1)
            def _(i):
                @pl.when(i < count)
                def _():
                    hop(0, c, i // PIECES, i % PIECES).wait_recv()
                    hop(1, c, i // PIECES, i % PIECES).start()

                @pl.when(i >= 1)
                def _():
                    hop(1, c, (i - 1) // PIECES, (i - 1) % PIECES).wait_recv()
                    hop(2, c, (i - 1) // PIECES, (i - 1) % PIECES).start()

        @pl.when(takes_part(reached + 2))
        def _():
            @pl.loop(0, count)
            def _(i):
                k, h = i // PIECES, i % PIECES
                hop(2, c, k, h).wait_recv()

                @pl.when(at_bottom)
                def _():
                    hop(3, c, k, h, 1).start()

                @pl.when(at_top)
                def _():
                    hop(3, c, k, h, 2).start()

    @pl.when(first)
    def _():
        for c in range(spans):
            for k in range(nc):
                for h in range(PIECES):
                    load_feats(c, k, h).start()

    load_tiles = pltpu.make_async_copy(tiles, tile_buf, tile_sem)
    load_tiles.start()
    for k in range(nc):
        load_w1(k).start()
        load_w2(k).start()

    barrier = pltpu.get_barrier_semaphore()
    pl.semaphore_signal(barrier, inc=1, device_id=above, device_id_type=MESH)
    pl.semaphore_signal(barrier, inc=1, device_id=below, device_id_type=MESH)

    @pl.when(jnp.logical_not(last))
    def _():
        pl.semaphore_signal(barrier, inc=1, device_id=after, device_id_type=MESH)

    @pl.when(jnp.logical_not(first))
    def _():
        pl.semaphore_signal(barrier, inc=1, device_id=before, device_id_type=MESH)

    extra = [q for q in sorted(set(helpers) - {1}) if section_count != 4]
    for q in extra:
        @pl.when(jnp.logical_and(first, edge))
        def _():
            pl.semaphore_signal(
                barrier, inc=1, device_id={"section": jnp.int32(q)}, device_id_type=MESH
            )

        @pl.when(jnp.logical_and(s == q, edge))
        def _():
            pl.semaphore_signal(
                barrier, inc=1, device_id={"section": jnp.int32(0)}, device_id_type=MESH
            )

    if section_count == 4:
        @pl.when(edge)
        def _():
            pl.semaphore_signal(barrier, inc=1, device_id=opposite, device_id_type=MESH)

    def one_if(condition):
        return jnp.where(condition, 1, 0).astype(jnp.int32)

    peers = 2 + one_if(jnp.logical_not(first)) + one_if(jnp.logical_not(last))
    for q in extra:
        peers += one_if(jnp.logical_and(jnp.logical_or(first, s == q), edge))
    if section_count == 4:
        peers += one_if(edge)
    pl.semaphore_wait(barrier, peers)

    def forward(c, k):
        for h in range(PIECES):
            @pl.when(first)
            def _():
                load_feats(c, k, h).wait()

            @pl.when(jnp.logical_not(first))
            def _():
                to_next(c, k, h).wait_recv()

            @pl.when(sends_above(c))
            def _():
                to_above(c, k, h).start()

            @pl.when(sends_below(c))
            def _():
                to_below(c, k, h).start()

    @pl.when(first)
    def _():
        for k in range(nc):
            forward(0, k)

    for c in range(spans):
        @pl.when(jnp.logical_and(s == helpers[c], edge))
        def _():
            @pl.loop(0, nc * PIECES)
            def _(i):
                across(c, i // PIECES, i % PIECES).start()

            @pl.loop(0, nc * PIECES)
            def _(i):
                k, h = i // PIECES, i % PIECES
                across(c, k, h).wait_recv()

                @pl.when(at_bottom)
                def _():
                    back(c, k, h, 1).start()

                @pl.when(at_top)
                def _():
                    back(c, k, h, 2).start()

    load_tiles.wait()

    def build(c):
        blocks = (c + 1) * 3 * blk_rows

        @pl.loop(0, blk_rows)
        def _(r):
            @pl.loop(0, blocks)
            def _(n):
                total = jnp.zeros((tile_len, tile_len), jnp.float32)
                for j in range(tiles_row):
                    hit = jnp.where(cols[c, r * tiles_row + j] == n, 1.0, 0.0)
                    total += tile_buf[c, r, j].astype(jnp.float32) * hit
                dense[
                    c,
                    pl.ds(pl.multiple_of(r * tile_len, tile_len), tile_len),
                    pl.ds(pl.multiple_of(n * tile_len, tile_len), tile_len),
                ] = total.astype(jnp.bfloat16)

    build(0)

    @pl.when(jnp.logical_not(first))
    def _():
        for c in range(1, spans):
            build(c)

    for k in range(nc):
        load_w1(k).wait()
        load_w2(k).wait()

    for c, reached in rerouted[:1]:
        pass_on(c, reached)

    def finish(c, k):
        for h in range(PIECES):
            to_above(c, k, h).wait_recv()
            to_below(c, k, h).wait_recv()
        start = (3 * c + 1) * rows
        total = agg[...] + jnp.dot(
            dense[c, :, start:start + 2 * rows],
            src[c, k, 1:3].reshape(2 * rows, CHUNK),
            preferred_element_type=jnp.float32,
        )
        acc[...] += jnp.dot(
            total.astype(jnp.bfloat16), w1_buf[k], preferred_element_type=jnp.float32
        )

    def begin(c, k):
        total = jnp.dot(
            dense[c, :, 3 * c * rows:(3 * c + 1) * rows],
            src[c, k, 0],
            preferred_element_type=jnp.float32,
        )
        for e in range(c):
            total += jnp.dot(
                dense[c, :, 3 * e * rows:3 * (e + 1) * rows],
                src[e, k].reshape(3 * rows, CHUNK),
                preferred_element_type=jnp.float32,
            )
        agg[...] = total

    for c in range(spans):
        if c > 0:
            @pl.when(first)
            def _():
                build(c)

        acc[...] = jnp.zeros_like(acc)

        @pl.loop(0, nc + 1)
        def _(k):
            @pl.when(jnp.logical_and(jnp.logical_not(first), k < nc))
            def _():
                forward(c, k)

            @pl.when(k >= 1)
            def _():
                finish(c, k - 1)

            @pl.when(k < nc)
            def _():
                begin(c, k)

        if c + 1 < spans:

            @pl.when(first)
            def _():
                for k in range(nc):
                    forward(c + 1, k)

        hidden[...] = jnp.maximum(acc[...], 0.0).astype(jnp.bfloat16)

        @pl.loop(0, nc)
        def _(k):
            updated = src[c, k, 0].astype(jnp.float32) + jnp.dot(
                hidden[...], w2_buf[k], preferred_element_type=jnp.float32
            )
            out_buf[c, k] = updated.astype(jnp.bfloat16)

            for span, reached in rerouted:
                if span == c:
                    @pl.when(takes_part(reached - 1))
                    def _():
                        for h in range(PIECES):
                            hop(0, c, k, h).start()

            @pl.when(jnp.logical_not(last))
            def _():
                for h in range(PIECES):
                    to_next(c, k, h).start()

            store_out(c, k).start()

    for c, reached in rerouted[1:]:
        pass_on(c, reached)

    for c in range(spans):
        @pl.loop(0, nc)
        def _(k):
            store_out(c, k).wait()
            for h in range(PIECES):
                @pl.when(sends_above(c))
                def _():
                    to_above(c, k, h).wait_send()

                @pl.when(sends_below(c))
                def _():
                    to_below(c, k, h).wait_send()

                @pl.when(jnp.logical_and(s == helpers[c], edge))
                def _():
                    across(c, k, h).wait_send()
                    back(c, k, h, 1).wait_send()

                @pl.when(jnp.logical_not(last))
                def _():
                    to_next(c, k, h).wait_send()

    for c, reached in rerouted:
        @pl.loop(0, nc)
        def _(k):
            for h in range(PIECES):
                @pl.when(takes_part(reached - 1))
                def _():
                    hop(0, c, k, h).wait_send()

                @pl.when(takes_part(reached + 1))
                def _():
                    hop(1, c, k, h).wait_send()
                    hop(2, c, k, h).wait_send()

                @pl.when(takes_part(reached + 2))
                def _():
                    hop(3, c, k, h).wait_send()


def on_device(features, tiles, w_first, w_second, tile_block):
    spans, rows, feat = features.shape
    blk_rows, tiles_row, tile_len = tiles.shape[1:4]
    section_count = lax.axis_size("section")
    part_count = lax.axis_size("dom")
    nc = feat // CHUNK
    cols = source_columns(tile_block, lax.axis_index("dom"), part_count, blk_rows)
    chunk_sems = pltpu.SemaphoreType.DMA((spans, nc, PIECES))
    bf16 = jnp.bfloat16
    anywhere = pl.BlockSpec(memory_space=pl.ANY)
    return pl.pallas_call(
        functools.partial(kernel, section_count, part_count, spans, nc),
        out_shape=jax.ShapeDtypeStruct((1, spans, rows, feat), bf16),
        in_specs=[pl.BlockSpec(memory_space=pltpu.SMEM)] + [anywhere] * 4,
        out_specs=anywhere,
        scratch_shapes=[
            pltpu.VMEM((spans, nc, 3, rows, CHUNK), bf16),
            pltpu.VMEM((spans, rows, spans * 3 * rows), bf16),
            pltpu.VMEM(tiles.shape, bf16),
            pltpu.VMEM((nc, CHUNK, feat), bf16),
            pltpu.VMEM((nc, feat, CHUNK), bf16),
            pltpu.VMEM((rows, CHUNK), jnp.float32),
            pltpu.VMEM((rows, feat), jnp.float32),
            pltpu.VMEM((rows, feat), bf16),
            pltpu.VMEM((spans, nc, rows, CHUNK), bf16),
            pltpu.VMEM((spans, nc, rows, CHUNK), bf16),
            pltpu.VMEM((3, nc, rows, CHUNK), bf16),
            chunk_sems,
            pltpu.SemaphoreType.DMA,
            pltpu.SemaphoreType.DMA((nc,)),
            pltpu.SemaphoreType.DMA((nc,)),
            pltpu.SemaphoreType.DMA((spans, nc)),
        ]
        + [chunk_sems] * 9
        + [pltpu.SemaphoreType.DMA((4, nc, PIECES)), pltpu.SemaphoreType.DMA((3, nc, PIECES))],
        compiler_params=pltpu.CompilerParams(
            collective_id=0, has_side_effects=True, vmem_limit_bytes=48 * 2**20
        ),
    )(cols, features, tiles, w_first, w_second)


def solution(mesh):
    placed = (
        P(None, "dom", None),
        P(None, "dom", None, None, None),
        P("section", None, None),
        P("section", None, None),
        P(),
    )
    return jax.shard_map(
        on_device,
        mesh=mesh,
        in_specs=placed,
        out_specs=P("section", None, "dom", None),
        check_vma=False,
    )
```

```python
import functools

import jax
import jax.numpy as jnp
from jax import lax
from jax.experimental import pallas as pl
from jax.experimental.pallas import tpu as pltpu
from jax.sharding import PartitionSpec as P

MESH = pl.DeviceIdType.MESH
CHUNK = 256
PIECES = 2


def source_columns(tile_block, my_part, part_count, blk_rows):
    spans, nbc, _ = tile_block.shape
    ids = lax.dynamic_slice_in_dim(tile_block, my_part * blk_rows, blk_rows, 1)
    ids = ids.reshape(spans, -1)
    within = ids % nbc
    offset_val = (within // blk_rows - my_part) % part_count
    side = jnp.where(offset_val == part_count - 1, 1, jnp.where(offset_val == 1, 2, 0))
    return ((ids // nbc) * 3 + side) * blk_rows + within % blk_rows


def kernel(
    section_count, part_count, spans, nc,
    cols, feats, tiles, w_first, w_second, out,
    src, dense, tile_buf, w1_buf, w2_buf, agg, acc, hidden, out_buf, relay, hop_buf,
    feat_sem, tile_sem, w1_sem, w2_sem, out_sem,
    next_send, own_recv, up_send, low_recv, down_send, high_recv,
    wrap_send, wrap_recv, back_send, hop_send, hop_recv,
):
    blk_rows, tiles_row, tile_len = tiles.shape[1:4]
    rows = blk_rows * tile_len
    s = lax.axis_index("section")
    p = lax.axis_index("dom")
    after = {"section": lax.rem(s + 1, section_count)}
    before = {"section": lax.rem(s + section_count - 1, section_count)}
    above = {"dom": lax.rem(p + 1, part_count)}
    below = {"dom": lax.rem(p + part_count - 1, part_count)}
    first = s == 0
    last = s == section_count - 1
    at_bottom = p == 0
    at_top = p == part_count - 1
    edge = jnp.logical_or(at_bottom, at_top)
    helpers = [1 + c % (section_count - 1) for c in range(spans)]
    rerouted = [(0, 1), (spans - 1, section_count - 1)] if section_count == 4 else []
    opposite = {"section": lax.rem(s + 2, section_count)}
    far_end = {"dom": jnp.where(at_bottom, part_count - 1, 0)}

    half = nc // 2

    def direct(c, k):
        found = jnp.logical_not(first)
        for span, reached in rerouted:
            if span == c:
                found = jnp.logical_and(found, jnp.logical_or(s != reached, k >= half))
        return found

    def sends_above(c, k):
        return jnp.logical_or(direct(c, k), jnp.logical_not(at_top))

    def sends_below(c, k):
        return jnp.logical_or(direct(c, k), jnp.logical_not(at_bottom))


    def columns(k):
        return pl.ds(pl.multiple_of(k * CHUNK, CHUNK), CHUNK)

    piece_rows = rows // PIECES

    def piece(h):
        return pl.ds(pl.multiple_of(h * piece_rows, piece_rows), piece_rows)

    def load_feats(c, k, h):
        return pltpu.make_async_copy(
            feats.at[c, piece(h), columns(k)], src.at[c, k, 0, piece(h)], feat_sem.at[c, k, h]
        )

    def load_w1(k):
        return pltpu.make_async_copy(
            w_first.at[0, pl.ds(pl.multiple_of(k * CHUNK, CHUNK), CHUNK)],
            w1_buf.at[k],
            w1_sem.at[k],
        )

    def load_w2(k):
        return pltpu.make_async_copy(
            w_second.at[0, :, columns(k)], w2_buf.at[k], w2_sem.at[k]
        )

    def store_out(c, k):
        return pltpu.make_async_copy(
            out_buf.at[c, k], out.at[0, c, :, columns(k)], out_sem.at[c, k]
        )

    def to_next(c, k, h):
        return pltpu.make_async_remote_copy(
            src_ref=out_buf.at[c, k, piece(h)],
            dst_ref=src.at[c, k, 0, piece(h)],
            send_sem=next_send.at[c, k, h],
            recv_sem=own_recv.at[c, k, h],
            device_id=after,
            device_id_type=MESH,
        )

    def to_above(c, k, h):
        return pltpu.make_async_remote_copy(
            src_ref=src.at[c, k, 0, piece(h)],
            dst_ref=src.at[c, k, 1, piece(h)],
            send_sem=up_send.at[c, k, h],
            recv_sem=low_recv.at[c, k, h],
            device_id=above,
            device_id_type=MESH,
        )

    def to_below(c, k, h):
        return pltpu.make_async_remote_copy(
            src_ref=src.at[c, k, 0, piece(h)],
            dst_ref=src.at[c, k, 2, piece(h)],
            send_sem=down_send.at[c, k, h],
            recv_sem=high_recv.at[c, k, h],
            device_id=below,
            device_id_type=MESH,
        )

    def across(c, k, h):
        return pltpu.make_async_remote_copy(
            src_ref=feats.at[c, piece(h), columns(k)],
            dst_ref=relay.at[c, k, piece(h)],
            send_sem=wrap_send.at[c, k, h],
            recv_sem=wrap_recv.at[c, k, h],
            device_id=far_end,
            device_id_type=MESH,
        )

    def back(c, k, h, side):
        return pltpu.make_async_remote_copy(
            src_ref=relay.at[c, k, piece(h)],
            dst_ref=src.at[c, k, side, piece(h)],
            send_sem=back_send.at[c, k, h],
            recv_sem=(low_recv if side == 1 else high_recv).at[c, k, h],
            device_id={"section": jnp.int32(0)},
            device_id_type=MESH,
        )

    def hop(n, c, k, h, side=1):
        source = out_buf.at[c, k, piece(h)] if n == 0 else hop_buf.at[n - 1, k, piece(h)]
        if n < 3:
            target, arrival = hop_buf.at[n, k, piece(h)], hop_recv.at[n, k, h]
        else:
            target = src.at[c, k, side, piece(h)]
            arrival = (low_recv if side == 1 else high_recv).at[c, k, h]
        return pltpu.make_async_remote_copy(
            src_ref=source,
            dst_ref=target,
            send_sem=hop_send.at[n, k, h],
            recv_sem=arrival,
            device_id=(opposite, far_end, after, opposite)[n],
            device_id_type=MESH,
        )

    def takes_part(section):
        return jnp.logical_and(s == section % section_count, edge)

    def pass_on(c, reached):
        count = half * PIECES

        @pl.when(takes_part(reached + 1))
        def _():
            @pl.loop(0, count + 1)
            def _(i):
                @pl.when(i < count)
                def _():
                    hop(0, c, i // PIECES, i % PIECES).wait_recv()
                    hop(1, c, i // PIECES, i % PIECES).start()

                @pl.when(i >= 1)
                def _():
                    hop(1, c, (i - 1) // PIECES, (i - 1) % PIECES).wait_recv()
                    hop(2, c, (i - 1) // PIECES, (i - 1) % PIECES).start()

        @pl.when(takes_part(reached + 2))
        def _():
            @pl.loop(0, count)
            def _(i):
                k, h = i // PIECES, i % PIECES
                hop(2, c, k, h).wait_recv()

                @pl.when(at_bottom)
                def _():
                    hop(3, c, k, h, 1).start()

                @pl.when(at_top)
                def _():
                    hop(3, c, k, h, 2).start()

    @pl.when(first)
    def _():
        for c in range(spans):
            for k in range(nc):
                for h in range(PIECES):
                    load_feats(c, k, h).start()

    load_tiles = pltpu.make_async_copy(tiles, tile_buf, tile_sem)
    load_tiles.start()
    for k in range(nc):
        load_w1(k).start()
        load_w2(k).start()

    barrier = pltpu.get_barrier_semaphore()
    pl.semaphore_signal(barrier, inc=1, device_id=above, device_id_type=MESH)
    pl.semaphore_signal(barrier, inc=1, device_id=below, device_id_type=MESH)

    @pl.when(jnp.logical_not(last))
    def _():
        pl.semaphore_signal(barrier, inc=1, device_id=after, device_id_type=MESH)

    @pl.when(jnp.logical_not(first))
    def _():
        pl.semaphore_signal(barrier, inc=1, device_id=before, device_id_type=MESH)

    extra = [q for q in sorted(set(helpers) - {1}) if section_count != 4]
    for q in extra:
        @pl.when(jnp.logical_and(first, edge))
        def _():
            pl.semaphore_signal(
                barrier, inc=1, device_id={"section": jnp.int32(q)}, device_id_type=MESH
            )

        @pl.when(jnp.logical_and(s == q, edge))
        def _():
            pl.semaphore_signal(
                barrier, inc=1, device_id={"section": jnp.int32(0)}, device_id_type=MESH
            )

    if section_count == 4:
        @pl.when(edge)
        def _():
            pl.semaphore_signal(barrier, inc=1, device_id=opposite, device_id_type=MESH)

    def one_if(condition):
        return jnp.where(condition, 1, 0).astype(jnp.int32)

    peers = 2 + one_if(jnp.logical_not(first)) + one_if(jnp.logical_not(last))
    for q in extra:
        peers += one_if(jnp.logical_and(jnp.logical_or(first, s == q), edge))
    if section_count == 4:
        peers += one_if(edge)
    pl.semaphore_wait(barrier, peers)

    def forward(c, k):
        for h in range(PIECES):
            @pl.when(first)
            def _():
                load_feats(c, k, h).wait()

            @pl.when(jnp.logical_not(first))
            def _():
                to_next(c, k, h).wait_recv()

            @pl.when(sends_above(c, k))
            def _():
                to_above(c, k, h).start()

            @pl.when(sends_below(c, k))
            def _():
                to_below(c, k, h).start()

    @pl.when(first)
    def _():
        for k in range(nc):
            forward(0, k)

    for c in range(spans):
        @pl.when(jnp.logical_and(s == helpers[c], edge))
        def _():
            @pl.loop(0, nc * PIECES)
            def _(i):
                across(c, i // PIECES, i % PIECES).start()

            @pl.loop(0, nc * PIECES)
            def _(i):
                k, h = i // PIECES, i % PIECES
                across(c, k, h).wait_recv()

                @pl.when(at_bottom)
                def _():
                    back(c, k, h, 1).start()

                @pl.when(at_top)
                def _():
                    back(c, k, h, 2).start()

    load_tiles.wait()

    def build(c):
        blocks = (c + 1) * 3 * blk_rows

        @pl.loop(0, blk_rows)
        def _(r):
            @pl.loop(0, blocks)
            def _(n):
                total = jnp.zeros((tile_len, tile_len), jnp.float32)
                for j in range(tiles_row):
                    hit = jnp.where(cols[c, r * tiles_row + j] == n, 1.0, 0.0)
                    total += tile_buf[c, r, j].astype(jnp.float32) * hit
                dense[
                    c,
                    pl.ds(pl.multiple_of(r * tile_len, tile_len), tile_len),
                    pl.ds(pl.multiple_of(n * tile_len, tile_len), tile_len),
                ] = total.astype(jnp.bfloat16)

    build(0)

    @pl.when(jnp.logical_not(first))
    def _():
        for c in range(1, spans):
            build(c)

    for k in range(nc):
        load_w1(k).wait()
        load_w2(k).wait()

    for c, reached in rerouted[:1]:
        pass_on(c, reached)

    def finish(c, k):
        for h in range(PIECES):
            to_above(c, k, h).wait_recv()
            to_below(c, k, h).wait_recv()
        start = (3 * c + 1) * rows
        total = agg[...] + jnp.dot(
            dense[c, :, start:start + 2 * rows],
            src[c, k, 1:3].reshape(2 * rows, CHUNK),
            preferred_element_type=jnp.float32,
        )
        acc[...] += jnp.dot(
            total.astype(jnp.bfloat16), w1_buf[k], preferred_element_type=jnp.float32
        )

    def begin(c, k):
        total = jnp.dot(
            dense[c, :, 3 * c * rows:(3 * c + 1) * rows],
            src[c, k, 0],
            preferred_element_type=jnp.float32,
        )
        for e in range(c):
            total += jnp.dot(
                dense[c, :, 3 * e * rows:3 * (e + 1) * rows],
                src[e, k].reshape(3 * rows, CHUNK),
                preferred_element_type=jnp.float32,
            )
        agg[...] = total

    for c in range(spans):
        if c > 0:
            @pl.when(first)
            def _():
                build(c)

        acc[...] = jnp.zeros_like(acc)

        @pl.loop(0, nc + 1)
        def _(k):
            @pl.when(jnp.logical_and(jnp.logical_not(first), k < nc))
            def _():
                forward(c, k)

            @pl.when(k >= 1)
            def _():
                finish(c, k - 1)

            @pl.when(k < nc)
            def _():
                begin(c, k)

        if c + 1 < spans:

            @pl.when(first)
            def _():
                for k in range(nc):
                    forward(c + 1, k)

        hidden[...] = jnp.maximum(acc[...], 0.0).astype(jnp.bfloat16)

        @pl.loop(0, nc)
        def _(k):
            updated = src[c, k, 0].astype(jnp.float32) + jnp.dot(
                hidden[...], w2_buf[k], preferred_element_type=jnp.float32
            )
            out_buf[c, k] = updated.astype(jnp.bfloat16)

            for span, reached in rerouted:
                if span == c:
                    @pl.when(jnp.logical_and(takes_part(reached - 1), k < half))
                    def _():
                        for h in range(PIECES):
                            hop(0, c, k, h).start()

            @pl.when(jnp.logical_not(last))
            def _():
                for h in range(PIECES):
                    to_next(c, k, h).start()

            store_out(c, k).start()

    for c, reached in rerouted[1:]:
        pass_on(c, reached)

    for c in range(spans):
        @pl.loop(0, nc)
        def _(k):
            store_out(c, k).wait()
            for h in range(PIECES):
                @pl.when(sends_above(c, k))
                def _():
                    to_above(c, k, h).wait_send()

                @pl.when(sends_below(c, k))
                def _():
                    to_below(c, k, h).wait_send()

                @pl.when(jnp.logical_and(s == helpers[c], edge))
                def _():
                    across(c, k, h).wait_send()
                    back(c, k, h, 1).wait_send()

                @pl.when(jnp.logical_not(last))
                def _():
                    to_next(c, k, h).wait_send()

    for c, reached in rerouted:
        @pl.loop(0, half)
        def _(k):
            for h in range(PIECES):
                @pl.when(takes_part(reached - 1))
                def _():
                    hop(0, c, k, h).wait_send()

                @pl.when(takes_part(reached + 1))
                def _():
                    hop(1, c, k, h).wait_send()
                    hop(2, c, k, h).wait_send()

                @pl.when(takes_part(reached + 2))
                def _():
                    hop(3, c, k, h).wait_send()


def on_device(features, tiles, w_first, w_second, tile_block):
    spans, rows, feat = features.shape
    blk_rows, tiles_row, tile_len = tiles.shape[1:4]
    section_count = lax.axis_size("section")
    part_count = lax.axis_size("dom")
    nc = feat // CHUNK
    cols = source_columns(tile_block, lax.axis_index("dom"), part_count, blk_rows)
    chunk_sems = pltpu.SemaphoreType.DMA((spans, nc, PIECES))
    bf16 = jnp.bfloat16
    anywhere = pl.BlockSpec(memory_space=pl.ANY)
    return pl.pallas_call(
        functools.partial(kernel, section_count, part_count, spans, nc),
        out_shape=jax.ShapeDtypeStruct((1, spans, rows, feat), bf16),
        in_specs=[pl.BlockSpec(memory_space=pltpu.SMEM)] + [anywhere] * 4,
        out_specs=anywhere,
        scratch_shapes=[
            pltpu.VMEM((spans, nc, 3, rows, CHUNK), bf16),
            pltpu.VMEM((spans, rows, spans * 3 * rows), bf16),
            pltpu.VMEM(tiles.shape, bf16),
            pltpu.VMEM((nc, CHUNK, feat), bf16),
            pltpu.VMEM((nc, feat, CHUNK), bf16),
            pltpu.VMEM((rows, CHUNK), jnp.float32),
            pltpu.VMEM((rows, feat), jnp.float32),
            pltpu.VMEM((rows, feat), bf16),
            pltpu.VMEM((spans, nc, rows, CHUNK), bf16),
            pltpu.VMEM((spans, nc, rows, CHUNK), bf16),
            pltpu.VMEM((3, nc, rows, CHUNK), bf16),
            chunk_sems,
            pltpu.SemaphoreType.DMA,
            pltpu.SemaphoreType.DMA((nc,)),
            pltpu.SemaphoreType.DMA((nc,)),
            pltpu.SemaphoreType.DMA((spans, nc)),
        ]
        + [chunk_sems] * 9
        + [pltpu.SemaphoreType.DMA((4, nc, PIECES)), pltpu.SemaphoreType.DMA((3, nc, PIECES))],
        compiler_params=pltpu.CompilerParams(
            collective_id=0, has_side_effects=True, vmem_limit_bytes=48 * 2**20
        ),
    )(cols, features, tiles, w_first, w_second)


def solution(mesh):
    placed = (
        P(None, "dom", None),
        P(None, "dom", None, None, None),
        P("section", None, None),
        P("section", None, None),
        P(),
    )
    return jax.shard_map(
        on_device,
        mesh=mesh,
        in_specs=placed,
        out_specs=P("section", None, "dom", None),
        check_vma=False,
    )
```
